32 devices in a mesh: dp: 2 (over y), expert: 16 (over z, x, core).
Axes of the slice: x: 2, y: 2, z: 4, core: 2. Of those that a mesh axis runs over, the one named last changes fastest.
Arguments:
- tokens: bfloat16 [1024, 2048], P(('dp', 'expert')), may hold values from -6 to 6
- routes: int32 [1024, 8], P(('dp', 'expert')), may hold values from 0 to 15, all different within a row; in each aligned block of 32 rows (0 to 31, 32 to 63, ...) at most 32 rows name the same one
- cotangent: bfloat16 [1024, 2048], P(('dp', 'expert')), may hold values from -6 to 6
- router_weight: bfloat16 [2048, 16], replicated, may hold values from -0.375 to 0.375
- gate_weight: bfloat16 [16, 2048, 768], P('expert'), may hold values from -0.125 to 0.125
- up_weight: bfloat16 [16, 2048, 768], P('expert'), may hold values from -0.125 to 0.125
- down_weight: bfloat16 [16, 768, 2048], P('expert'), may hold values from -0.21875 to 0.21875
Outputs:
- layer_out: bfloat16 [1024, 2048], P(('dp', 'expert'))
- token_grad: bfloat16 [1024, 2048], P(('dp', 'expert'))
- gate_grad: bfloat16 [16, 2048, 768], P('expert', 'dp')
- up_grad: bfloat16 [16, 2048, 768], P('expert', 'dp')
- down_grad: bfloat16 [16, 768, 2048], P('expert', None, 'dp')
- router_grad: float32 [2048, 16], replicated
The draws below stay inside these ranges and needn't reach their ends.
Inputs may be any that keep to these rules, and one draw needn't show every extreme that they name: `routes`: each row names 8 different experts. Among the 32 rows of one device no expert is named by more than 32 rows, and in some device's rows an expert is named by exactly 32 rows.
All inputs are finite; a program needn't handle non-finite values.
Results may differ from the reference program's by a relative error of at most 0.0061.
Values may be sent and summed in bfloat16 or wider, within the bound.
A program may use at most 128 MiB of HBM per device.

```python
import math
import jax
import jax.numpy as jnp
import numpy as np
from jax import lax

D = 2048
F = 768
TOPK = 8
TOK_DEV = 32
EXPERTS = 16
CAP = 32
TOKENS = 1024


def levels(rng, extent, cuts, least, high):
    gain = 1.0
    for axis_at, blocks in cuts:
        heights = jax.random.uniform(jax.random.fold_in(jax.random.fold_in(rng, 6), axis_at), (blocks,), jnp.float32, least / len(cuts), high / len(cuts))
        gain = gain * jnp.repeat(jnp.exp(heights), extent[axis_at] // blocks).reshape((-1,) + (1,) * (len(extent) - 1 - axis_at))
    return gain


def deal_out(stream_key, own, number, rows, amount, top, bound, lean):
    sequence = jax.random.permutation(stream_key, amount)
    crowded, ordinary = portions_of(amount, rows * top, bound, lean, True), portions_of(amount, rows * top, bound, lean, False)
    places = jnp.arange(amount)

    def named(sizes, rotation):
        used = int((sizes > 0).sum())
        fixed = max(1, used // 4)
        shifted = fixed + (places - fixed + rotation * (used - fixed)) % max(1, amount - fixed)
        return jnp.zeros((amount,), jnp.int32).at[sequence[jnp.where(places < fixed, places, shifted)]].set(jnp.asarray(sizes, jnp.int32))

    sizes = jnp.where(number % 4 == 0, named(crowded, number // 4), named(ordinary, number - number // 4 - 1))
    mixed = jax.random.permutation(jax.random.fold_in(own, 3), amount)
    donor, sink = mixed[0:amount // 2 * 2:2], mixed[1:amount // 2 * 2:2]
    slack = jnp.minimum(sizes[donor] - 1, bound - sizes[sink]) // 2
    slack = jnp.where((donor == sequence[0]) | (sink == sequence[0]) | (sizes[sink] == 0), 0, jnp.maximum(slack, 0))
    shifted = jax.random.randint(jax.random.fold_in(own, 4), (amount // 2,), 0, 1 << 20) % (slack + 1)
    sizes = sizes.at[donor].add(-shifted).at[sink].add(shifted)
    members = jnp.searchsorted(jnp.cumsum(sizes), jnp.arange(rows * top), side="right").astype(jnp.int32)
    grid = members.reshape(top, rows).T
    grid = grid[jax.random.permutation(jax.random.fold_in(own, 1), rows)]
    rotation = jax.random.randint(jax.random.fold_in(own, 2), (rows, 1), 0, top)
    return jnp.take_along_axis(grid, (jnp.arange(top)[None, :] + rotation) % top, axis=1)


def portions_of(number_of, total, limit, skew, full):
    loads = [(1 << 20) // math.isqrt(grade ** skew) + 1 for grade in range(1, number_of + 1)]
    largest = limit if full else min(limit, max(-(-total // number_of), total * loads[0] // sum(loads)))
    least = 1 if total - largest >= number_of - 1 else 0
    given, surplus = [largest] + [least] * (number_of - 1), total - largest - least * (number_of - 1)
    while surplus > 0:
        free = [i for i in range(1, number_of) if given[i] < largest] or [i for i in range(1, number_of) if given[i] < limit]
        pool, budget = sum([loads[i] for i in free]), surplus
        for i in free:
            more = min(limit - given[i], max(1, budget * loads[i] // pool), surplus)
            given[i] = given[i] + more
            surplus = surplus - more
    return np.array(given)


def scatter_about(own_key, shape, scale, limit, split=(), kind=jnp.bfloat16):
    drawn = scale * jax.random.normal(own_key, shape, jnp.float32)
    if split:
        drawn = drawn * levels(own_key, shape, split, -0.22, 0.18)
    return jnp.clip(drawn, -limit, limit).astype(kind)


def setup_inputs(seed: int = 0) -> dict:
    arg_keys = jax.random.split(jax.random.key(seed), 8)
    tokens = scatter_about(arg_keys[0], (TOKENS, D), 1.0, 6.0, ((0, 32),))
    routes_keys = jax.random.split(jax.random.fold_in(arg_keys[1], 1), TOKENS // TOK_DEV)
    routes_turns = jax.random.permutation(jax.random.fold_in(arg_keys[1], 3), TOKENS // TOK_DEV)
    routes = jax.vmap(lambda own, number: deal_out(jax.random.fold_in(arg_keys[1], 2), own, number, TOK_DEV, EXPERTS, TOPK, CAP, 2))(routes_keys, routes_turns).reshape((TOKENS, TOPK))
    cotangent = scatter_about(arg_keys[2], (TOKENS, D), 1.0, 6.0, ((0, 32),))
    router_weight = scatter_about(arg_keys[3], (D, EXPERTS), (D // 9) ** -0.5, 0.375)
    gate_weight = scatter_about(arg_keys[4], (EXPERTS, D, F), D ** -0.5, 0.125, ((0, 16),))
    up_weight = scatter_about(arg_keys[5], (EXPERTS, D, F), D ** -0.5, 0.125, ((0, 16),))
    down_weight = scatter_about(arg_keys[6], (EXPERTS, F, D), F ** -0.5, 0.21875, ((0, 16),))
    return {"tokens": tokens, "routes": routes, "cotangent": cotangent, "router_weight": router_weight, "gate_weight": gate_weight, "up_weight": up_weight, "down_weight": down_weight}


def silu_parts(gate_act):
    sigmoid_value = jax.nn.sigmoid(gate_act)
    act_value = gate_act * sigmoid_value
    act_slope = sigmoid_value * (1.0 + gate_act * (1.0 - sigmoid_value))
    return act_value, act_slope


def reference(tokens, routes, cotangent, router_weight, gate_weight, up_weight, down_weight):
    tok_all, top_count = routes.shape
    expert_count = router_weight.shape[1]
    blocks = tok_all // TOK_DEV
    pair_count = tok_all * top_count
    logits = jnp.dot(tokens, router_weight, preferred_element_type=jnp.float32)
    exp_logits = jnp.exp(logits)
    probability = exp_logits / jnp.sum(exp_logits, axis=1, keepdims=True)
    chosen = (routes[:, :, None] == jnp.arange(expert_count, dtype=jnp.int32)[None, None, :]).astype(jnp.int32)
    chosen_blocks = chosen.reshape(blocks, TOK_DEV, top_count, expert_count)
    per_token = jnp.sum(chosen_blocks, axis=2).astype(jnp.int32)
    earlier = (jnp.cumsum(per_token, axis=1) - per_token).astype(jnp.int32)
    slot_ids = jnp.sum(chosen_blocks * earlier[:, :, None, :], axis=3).astype(jnp.int32).reshape(tok_all, top_count)
    block_of = (jnp.arange(tok_all, dtype=jnp.int32) // TOK_DEV).astype(jnp.int32)
    position = ((routes * blocks + block_of[:, None]) * CAP + slot_ids).astype(jnp.int32)
    slot_table = jnp.full((expert_count * blocks * CAP,), pair_count, dtype=jnp.int32)
    slot_table = slot_table.at[position.reshape(-1)].set(jnp.arange(pair_count, dtype=jnp.int32))
    slot_table = slot_table.reshape(expert_count, blocks * CAP)
    chosen_float = chosen.astype(jnp.float32)
    selected = jnp.sum(chosen_float * probability[:, None, :], axis=2)
    sel_total = jnp.sum(selected, axis=1, keepdims=True)
    combine = selected / sel_total
    zero_row = jnp.zeros((1, D), tokens.dtype)
    tokens_pad = jnp.concatenate([tokens, zero_row], axis=0)
    cot_pad = jnp.concatenate([cotangent, zero_row], axis=0)
    combine_pad = jnp.concatenate([combine.reshape(-1), jnp.zeros((1,), jnp.float32)])

    def expert_step(running, inputs):
        mixed_acc, grad_acc, comb_acc = running
        row_ids, gate_mat, up_mat, down_mat = inputs
        token_ids = (row_ids // top_count).astype(jnp.int32)
        slot_inputs = tokens_pad[token_ids]
        slot_cot = cot_pad[token_ids]
        slot_comb = combine_pad[row_ids]
        slot_grads = (slot_comb[:, None] * slot_cot.astype(jnp.float32)).astype(jnp.bfloat16)
        gate_act = jnp.dot(slot_inputs, gate_mat, preferred_element_type=jnp.float32)
        up_act = jnp.dot(slot_inputs, up_mat, preferred_element_type=jnp.float32)
        act_value, act_slope = silu_parts(gate_act)
        hidden = (act_value * up_act).astype(jnp.bfloat16)
        expert_out = jnp.dot(hidden, down_mat, preferred_element_type=jnp.float32).astype(jnp.bfloat16)
        hidden_grad = jnp.dot(slot_grads, down_mat.T, preferred_element_type=jnp.float32)
        gate_part = (hidden_grad * up_act * act_slope).astype(jnp.bfloat16)
        up_part = (hidden_grad * act_value).astype(jnp.bfloat16)
        input_grad = (jnp.dot(gate_part, gate_mat.T, preferred_element_type=jnp.float32)
                      + jnp.dot(up_part, up_mat.T, preferred_element_type=jnp.float32)).astype(jnp.bfloat16)
        gate_part_sum = jnp.dot(slot_inputs.T, gate_part, preferred_element_type=jnp.float32).astype(jnp.bfloat16)
        up_part_sum = jnp.dot(slot_inputs.T, up_part, preferred_element_type=jnp.float32).astype(jnp.bfloat16)
        down_part_sum = jnp.dot(hidden.T, slot_grads, preferred_element_type=jnp.float32).astype(jnp.bfloat16)
        out_float = expert_out.astype(jnp.float32)
        mixed_acc = mixed_acc.at[token_ids].add(slot_comb[:, None] * out_float)
        grad_acc = grad_acc.at[token_ids].add(input_grad.astype(jnp.float32))
        comb_acc = comb_acc.at[row_ids].add(jnp.sum(slot_cot.astype(jnp.float32) * out_float, axis=1))
        return (mixed_acc, grad_acc, comb_acc), (gate_part_sum, up_part_sum, down_part_sum)

    start_state = (jnp.zeros((tok_all + 1, D), jnp.float32),
                   jnp.zeros((tok_all + 1, D), jnp.float32),
                   jnp.zeros((pair_count + 1,), jnp.float32))
    final_state, weight_grads = lax.scan(expert_step, start_state, (slot_table, gate_weight, up_weight, down_weight))
    mixed_acc, grad_acc, comb_acc = final_state
    gate_grad, up_grad, down_grad = weight_grads
    layer_out = mixed_acc[:tok_all].astype(jnp.bfloat16)
    comb_grad = comb_acc[:pair_count].reshape(tok_all, top_count)
    sel_grad = (comb_grad - jnp.sum(combine * comb_grad, axis=1, keepdims=True)) / sel_total
    prob_grad = jnp.sum(chosen_float * sel_grad[:, :, None], axis=1)
    logit_grad = probability * (prob_grad - jnp.sum(probability * prob_grad, axis=1, keepdims=True))
    router_grad = jnp.dot(tokens.astype(jnp.float32).T, logit_grad, precision=lax.Precision.HIGHEST)
    router_back = jnp.dot(logit_grad, router_weight.astype(jnp.float32).T, precision=lax.Precision.HIGHEST)
    token_grad = (grad_acc[:tok_all] + router_back).astype(jnp.bfloat16)
    return (layer_out, token_grad, gate_grad, up_grad, down_grad, router_grad)
```

```python
import jax
import jax.numpy as jnp
from jax import lax
from jax.sharding import PartitionSpec as P


def silu_parts(gate_act):
    sigmoid_value = jax.nn.sigmoid(gate_act)
    act_value = gate_act * sigmoid_value
    act_slope = sigmoid_value * (1.0 + gate_act * (1.0 - sigmoid_value))
    return (act_value, act_slope)


def expert_forward(arrived, gate_weight, up_weight, down_weight):
    gate_act = jnp.einsum(
        "sjcd,jdf->sjcf", arrived, gate_weight, preferred_element_type=jnp.float32
    )
    up_act = jnp.einsum("sjcd,jdf->sjcf", arrived, up_weight, preferred_element_type=jnp.float32)
    act_value, act_slope = silu_parts(gate_act)
    hidden = (act_value * up_act).astype(jnp.bfloat16)
    expert_out = jnp.einsum(
        "sjcf,jfd->sjcd", hidden, down_weight, preferred_element_type=jnp.float32
    ).astype(jnp.bfloat16)
    return (expert_out, (up_act, act_value, act_slope, hidden))


def expert_backward(arrived_grads, stored, gate_weight, up_weight, down_weight):
    up_act, act_value, act_slope, hidden = stored
    hidden_grad = jnp.einsum(
        "sjcd,jfd->sjcf", arrived_grads, down_weight, preferred_element_type=jnp.float32
    )
    gate_part = (hidden_grad * up_act * act_slope).astype(jnp.bfloat16)
    up_part = (hidden_grad * act_value).astype(jnp.bfloat16)
    input_grad = (
        jnp.einsum("sjcf,jdf->sjcd", gate_part, gate_weight, preferred_element_type=jnp.float32)
        + jnp.einsum("sjcf,jdf->sjcd", up_part, up_weight, preferred_element_type=jnp.float32)
    ).astype(jnp.bfloat16)
    return (input_grad, gate_part, up_part)


def local_slots(tokens, routes, cotangent, router_weight, gate_weight, up_weight, down_weight):
    tok_rows, top_count = routes.shape
    model_width = tokens.shape[1]
    expert_count = router_weight.shape[1]
    local_count = gate_weight.shape[0]
    group_size = lax.axis_size("expert")
    capacity = min(tok_rows, 2 * tok_rows * top_count // expert_count)
    slot_total = expert_count * capacity
    buffer_shape = (group_size, local_count, capacity, model_width)
    logits = jnp.dot(tokens, router_weight, preferred_element_type=jnp.float32)
    exp_logits = jnp.exp(logits)
    probability = exp_logits / jnp.sum(exp_logits, axis=1, keepdims=True)
    chosen = (
        routes[:, :, None] == jnp.arange(expert_count, dtype=jnp.int32)[None, None, :]
    ).astype(jnp.int32)
    chosen_float = chosen.astype(jnp.float32)
    selected = jnp.sum(chosen_float * probability[:, None, :], axis=2)
    sel_total = jnp.sum(selected, axis=1, keepdims=True)
    combine = selected / sel_total
    per_token = jnp.sum(chosen, axis=1)
    before = jnp.tril(jnp.ones((tok_rows, tok_rows), jnp.float32), -1)
    earlier = jnp.dot(before, per_token.astype(jnp.float32)).astype(jnp.int32)
    slot_ids = jnp.sum(chosen * earlier[:, None, :], axis=2)
    flat_slot = routes * capacity + slot_ids
    match_map = (
        flat_slot[:, :, None] == jnp.arange(slot_total, dtype=jnp.int32)[None, None, :]
    ).astype(jnp.float32)
    presence = jnp.sum(match_map, axis=1)
    weight_map = jnp.sum(match_map * combine[:, :, None], axis=1)
    send_rows = (
        jnp.einsum(
            "tr,td->rd", presence.astype(jnp.bfloat16), tokens, preferred_element_type=jnp.float32
        )
        .astype(jnp.bfloat16)
        .reshape(buffer_shape)
    )
    send_grads = (
        jnp.einsum(
            "tr,td->rd", weight_map, cotangent.astype(jnp.float32), precision=lax.Precision.HIGHEST
        )
        .astype(jnp.bfloat16)
        .reshape(buffer_shape)
    )
    arrived = lax.all_to_all(send_rows, "expert", split_axis=0, concat_axis=0, tiled=True)
    expert_out, stored = expert_forward(arrived, gate_weight, up_weight, down_weight)
    returned = lax.all_to_all(expert_out, "expert", split_axis=0, concat_axis=0, tiled=True)
    arrived_grads = lax.all_to_all(send_grads, "expert", split_axis=0, concat_axis=0, tiled=True)
    input_grad, gate_part, up_part = expert_backward(
        arrived_grads, stored, gate_weight, up_weight, down_weight
    )
    returned_grads = lax.all_to_all(input_grad, "expert", split_axis=0, concat_axis=0, tiled=True)
    hidden = stored[3]
    gate_term = jnp.einsum("sjcd,sjcf->jdf", arrived, gate_part, preferred_element_type=jnp.float32)
    up_term = jnp.einsum("sjcd,sjcf->jdf", arrived, up_part, preferred_element_type=jnp.float32)
    down_term = jnp.einsum(
        "sjcf,sjcd->jfd", hidden, arrived_grads, preferred_element_type=jnp.float32
    )
    gate_sum, up_sum, down_sum = (
        lax.psum_scatter(gate_term, "dp", scatter_dimension=1, tiled=True),
        lax.psum_scatter(up_term, "dp", scatter_dimension=1, tiled=True),
        lax.psum_scatter(down_term, "dp", scatter_dimension=2, tiled=True),
    )
    gate_grad = gate_sum.astype(jnp.bfloat16)
    up_grad = up_sum.astype(jnp.bfloat16)
    down_grad = down_sum.astype(jnp.bfloat16)
    flat_index = flat_slot.reshape(-1)
    out_sel = jnp.take(returned.reshape(slot_total, model_width), flat_index, axis=0).reshape(
        tok_rows, top_count, model_width
    )
    grad_sel = jnp.take(
        returned_grads.reshape(slot_total, model_width), flat_index, axis=0
    ).reshape(tok_rows, top_count, model_width)
    layer_out = jnp.sum(combine[:, :, None] * out_sel.astype(jnp.float32), axis=1).astype(
        jnp.bfloat16
    )
    comb_grad = jnp.einsum("tkd,td->tk", out_sel, cotangent, preferred_element_type=jnp.float32)
    sel_grad = (comb_grad - jnp.sum(combine * comb_grad, axis=1, keepdims=True)) / sel_total
    prob_grad = jnp.sum(chosen_float * sel_grad[:, :, None], axis=1)
    logit_grad = probability * (prob_grad - jnp.sum(probability * prob_grad, axis=1, keepdims=True))
    router_term = jnp.einsum(
        "td,te->de", tokens.astype(jnp.float32), logit_grad, precision=lax.Precision.HIGHEST
    )
    router_grad = lax.psum(router_term, ("dp", "expert"))
    router_back = jnp.einsum(
        "te,de->td", logit_grad, router_weight.astype(jnp.float32), precision=lax.Precision.HIGHEST
    )
    token_grad = (jnp.sum(grad_sel.astype(jnp.float32), axis=1) + router_back).astype(jnp.bfloat16)
    return (layer_out, token_grad, gate_grad, up_grad, down_grad, router_grad)


def local_dense(tokens, routes, cotangent, router_weight, gate_weight, up_weight, down_weight):
    tok_rows = tokens.shape[0]
    model_width = tokens.shape[1]
    expert_count = router_weight.shape[1]
    group_size = lax.axis_size("expert")
    dp_size = lax.axis_size("dp")
    dp_index = lax.axis_index("dp")
    expert_index = lax.axis_index("expert")
    both = ("dp", "expert")
    gate_mat, up_mat, down_mat = gate_weight[0], up_weight[0], down_weight[0]
    routes_all = lax.all_gather(routes, both, axis=0, tiled=True)
    tokens_all = lax.all_gather(tokens, both, axis=0, tiled=True)
    cot_all = lax.all_gather(cotangent, both, axis=0, tiled=True)
    logits = jnp.dot(tokens_all, router_weight, preferred_element_type=jnp.float32)
    exp_logits = jnp.exp(logits)
    probability = exp_logits / jnp.sum(exp_logits, axis=1, keepdims=True)
    chosen = jnp.sum(
        (
            routes_all[:, :, None] == jnp.arange(expert_count, dtype=jnp.int32)[None, None, :]
        ).astype(jnp.float32),
        axis=1,
    )
    selected = chosen * probability
    sel_total = jnp.sum(selected, axis=1, keepdims=True)
    combine = selected / sel_total
    mine = (jnp.arange(expert_count, dtype=jnp.int32) == expert_index).astype(jnp.float32)
    scale = jnp.sum(combine * mine[None, :], axis=1, keepdims=True)
    gate_act = jnp.dot(tokens_all, gate_mat, preferred_element_type=jnp.float32)
    up_act = jnp.dot(tokens_all, up_mat, preferred_element_type=jnp.float32)
    raw_grad = lax.dot_general(
        cot_all, down_mat, (((1,), (1,)), ((), ())), preferred_element_type=jnp.float32
    )
    act_value, act_slope = silu_parts(gate_act)
    hidden = act_value * up_act
    comb_mine = jnp.sum(hidden * raw_grad, axis=1)
    scaled_hidden = (hidden * scale).astype(jnp.bfloat16)
    hidden_grad = raw_grad * scale
    gate_part = (hidden_grad * up_act * act_slope).astype(jnp.bfloat16)
    up_part = (hidden_grad * act_value).astype(jnp.bfloat16)
    group_rows = group_size * tok_rows
    first = dp_index * group_rows

    def rows_of(array):
        return lax.dynamic_slice_in_dim(array, first, group_rows, axis=0)

    out_term = jnp.dot(
        rows_of(scaled_hidden), down_mat, preferred_element_type=jnp.float32
    ).astype(jnp.bfloat16)
    layer_out = lax.psum_scatter(out_term, "expert", scatter_dimension=0, tiled=True)
    in_term = (
        lax.dot_general(
            rows_of(gate_part), gate_mat, (((1,), (1,)), ((), ())),
            preferred_element_type=jnp.float32,
        )
        + lax.dot_general(
            rows_of(up_part), up_mat, (((1,), (1,)), ((), ())),
            preferred_element_type=jnp.float32,
        )
    ).astype(jnp.bfloat16)
    in_sum = lax.psum_scatter(in_term, "expert", scatter_dimension=0, tiled=True)
    part_width = model_width // dp_size
    start = dp_index * part_width
    tokens_part = lax.dynamic_slice_in_dim(tokens_all, start, part_width, axis=1)
    cot_part = lax.dynamic_slice_in_dim(cot_all, start, part_width, axis=1)
    over_rows = (((0,), (0,)), ((), ()))
    gate_grad = lax.dot_general(
        tokens_part, gate_part, over_rows, preferred_element_type=jnp.float32
    ).astype(jnp.bfloat16)
    up_grad = lax.dot_general(
        tokens_part, up_part, over_rows, preferred_element_type=jnp.float32
    ).astype(jnp.bfloat16)
    down_grad = lax.dot_general(
        scaled_hidden, cot_part, over_rows, preferred_element_type=jnp.float32
    ).astype(jnp.bfloat16)
    comb_grad = lax.all_gather(comb_mine, "expert", axis=0).T
    sel_grad = (
        chosen * (comb_grad - jnp.sum(combine * comb_grad, axis=1, keepdims=True)) / sel_total
    )
    logit_grad = probability * (sel_grad - jnp.sum(probability * sel_grad, axis=1, keepdims=True))
    router_grad = jnp.einsum(
        "td,te->de",
        tokens_all.astype(jnp.float32),
        logit_grad,
        precision=lax.Precision.HIGHEST,
    )
    own_first = (dp_index * group_size + expert_index) * tok_rows
    own_logit_grad = lax.dynamic_slice_in_dim(logit_grad, own_first, tok_rows, axis=0)
    router_back = jnp.einsum(
        "te,de->td",
        own_logit_grad,
        router_weight.astype(jnp.float32),
        precision=lax.Precision.HIGHEST,
    )
    token_grad = (in_sum.astype(jnp.float32) + router_back).astype(jnp.bfloat16)
    return (layer_out, token_grad, gate_grad[None], up_grad[None], down_grad[None], router_grad)


def local(tokens, routes, cotangent, router_weight, gate_weight, up_weight, down_weight):
    tok_rows, top_count = routes.shape
    capacity = min(tok_rows, 2 * tok_rows * top_count // router_weight.shape[1])
    dense = capacity == tok_rows and gate_weight.shape[0] == 1
    plan = local_dense if dense else local_slots
    return plan(tokens, routes, cotangent, router_weight, gate_weight, up_weight, down_weight)


def solution(mesh):
    return jax.shard_map(
        local,
        mesh=mesh,
        in_specs=(
            P(("dp", "expert"), None),
            P(("dp", "expert"), None),
            P(("dp", "expert"), None),
            P(),
            P("expert", None, None),
            P("expert", None, None),
            P("expert", None, None),
        ),
        out_specs=(
            P(("dp", "expert"), None),
            P(("dp", "expert"), None),
            P("expert", "dp", None),
            P("expert", "dp", None),
            P("expert", None, "dp"),
            P(),
        ),
        check_vma=False,
    )
```

```python
import jax
import jax.numpy as jnp
from jax import lax
from jax.sharding import PartitionSpec as P


def silu_parts(gate_act):
    sigmoid_value = jax.nn.sigmoid(gate_act)
    act_value = gate_act * sigmoid_value
    act_slope = sigmoid_value * (1.0 + gate_act * (1.0 - sigmoid_value))
    return (act_value, act_slope)


def expert_forward(arrived, gate_weight, up_weight, down_weight):
    gate_act = jnp.einsum(
        "sjcd,jdf->sjcf", arrived, gate_weight, preferred_element_type=jnp.float32
    )
    up_act = jnp.einsum("sjcd,jdf->sjcf", arrived, up_weight, preferred_element_type=jnp.float32)
    act_value, act_slope = silu_parts(gate_act)
    hidden = (act_value * up_act).astype(jnp.bfloat16)
    expert_out = jnp.einsum(
        "sjcf,jfd->sjcd", hidden, down_weight, preferred_element_type=jnp.float32
    ).astype(jnp.bfloat16)
    return (expert_out, (up_act, act_value, act_slope, hidden))


def expert_backward(arrived_grads, stored, gate_weight, up_weight, down_weight):
    up_act, act_value, act_slope, hidden = stored
    hidden_grad = jnp.einsum(
        "sjcd,jfd->sjcf", arrived_grads, down_weight, preferred_element_type=jnp.float32
    )
    gate_part = (hidden_grad * up_act * act_slope).astype(jnp.bfloat16)
    up_part = (hidden_grad * act_value).astype(jnp.bfloat16)
    input_grad = (
        jnp.einsum("sjcf,jdf->sjcd", gate_part, gate_weight, preferred_element_type=jnp.float32)
        + jnp.einsum("sjcf,jdf->sjcd", up_part, up_weight, preferred_element_type=jnp.float32)
    ).astype(jnp.bfloat16)
    return (input_grad, gate_part, up_part)


def local_slots(tokens, routes, cotangent, router_weight, gate_weight, up_weight, down_weight):
    tok_rows, top_count = routes.shape
    model_width = tokens.shape[1]
    expert_count = router_weight.shape[1]
    local_count = gate_weight.shape[0]
    group_size = lax.axis_size("expert")
    capacity = min(tok_rows, 2 * tok_rows * top_count // expert_count)
    slot_total = expert_count * capacity
    buffer_shape = (group_size, local_count, capacity, model_width)
    logits = jnp.dot(tokens, router_weight, preferred_element_type=jnp.float32)
    exp_logits = jnp.exp(logits)
    probability = exp_logits / jnp.sum(exp_logits, axis=1, keepdims=True)
    chosen = (
        routes[:, :, None] == jnp.arange(expert_count, dtype=jnp.int32)[None, None, :]
    ).astype(jnp.int32)
    chosen_float = chosen.astype(jnp.float32)
    selected = jnp.sum(chosen_float * probability[:, None, :], axis=2)
    sel_total = jnp.sum(selected, axis=1, keepdims=True)
    combine = selected / sel_total
    per_token = jnp.sum(chosen, axis=1)
    before = jnp.tril(jnp.ones((tok_rows, tok_rows), jnp.float32), -1)
    earlier = jnp.dot(before, per_token.astype(jnp.float32)).astype(jnp.int32)
    slot_ids = jnp.sum(chosen * earlier[:, None, :], axis=2)
    flat_slot = routes * capacity + slot_ids
    match_map = (
        flat_slot[:, :, None] == jnp.arange(slot_total, dtype=jnp.int32)[None, None, :]
    ).astype(jnp.float32)
    presence = jnp.sum(match_map, axis=1)
    weight_map = jnp.sum(match_map * combine[:, :, None], axis=1)
    send_rows = (
        jnp.einsum(
            "tr,td->rd", presence.astype(jnp.bfloat16), tokens, preferred_element_type=jnp.float32
        )
        .astype(jnp.bfloat16)
        .reshape(buffer_shape)
    )
    send_grads = (
        jnp.einsum(
            "tr,td->rd", weight_map, cotangent.astype(jnp.float32), precision=lax.Precision.HIGHEST
        )
        .astype(jnp.bfloat16)
        .reshape(buffer_shape)
    )
    arrived = lax.all_to_all(send_rows, "expert", split_axis=0, concat_axis=0, tiled=True)
    expert_out, stored = expert_forward(arrived, gate_weight, up_weight, down_weight)
    returned = lax.all_to_all(expert_out, "expert", split_axis=0, concat_axis=0, tiled=True)
    arrived_grads = lax.all_to_all(send_grads, "expert", split_axis=0, concat_axis=0, tiled=True)
    input_grad, gate_part, up_part = expert_backward(
        arrived_grads, stored, gate_weight, up_weight, down_weight
    )
    returned_grads = lax.all_to_all(input_grad, "expert", split_axis=0, concat_axis=0, tiled=True)
    hidden = stored[3]
    gate_term = jnp.einsum("sjcd,sjcf->jdf", arrived, gate_part, preferred_element_type=jnp.float32)
    up_term = jnp.einsum("sjcd,sjcf->jdf", arrived, up_part, preferred_element_type=jnp.float32)
    down_term = jnp.einsum(
        "sjcf,sjcd->jfd", hidden, arrived_grads, preferred_element_type=jnp.float32
    )
    gate_sum, up_sum, down_sum = (
        lax.psum_scatter(gate_term, "dp", scatter_dimension=1, tiled=True),
        lax.psum_scatter(up_term, "dp", scatter_dimension=1, tiled=True),
        lax.psum_scatter(down_term, "dp", scatter_dimension=2, tiled=True),
    )
    gate_grad = gate_sum.astype(jnp.bfloat16)
    up_grad = up_sum.astype(jnp.bfloat16)
    down_grad = down_sum.astype(jnp.bfloat16)
    flat_index = flat_slot.reshape(-1)
    out_sel = jnp.take(returned.reshape(slot_total, model_width), flat_index, axis=0).reshape(
        tok_rows, top_count, model_width
    )
    grad_sel = jnp.take(
        returned_grads.reshape(slot_total, model_width), flat_index, axis=0
    ).reshape(tok_rows, top_count, model_width)
    layer_out = jnp.sum(combine[:, :, None] * out_sel.astype(jnp.float32), axis=1).astype(
        jnp.bfloat16
    )
    comb_grad = jnp.einsum("tkd,td->tk", out_sel, cotangent, preferred_element_type=jnp.float32)
    sel_grad = (comb_grad - jnp.sum(combine * comb_grad, axis=1, keepdims=True)) / sel_total
    prob_grad = jnp.sum(chosen_float * sel_grad[:, :, None], axis=1)
    logit_grad = probability * (prob_grad - jnp.sum(probability * prob_grad, axis=1, keepdims=True))
    router_term = jnp.einsum(
        "td,te->de", tokens.astype(jnp.float32), logit_grad, precision=lax.Precision.HIGHEST
    )
    router_grad = lax.psum(router_term, ("dp", "expert"))
    router_back = jnp.einsum(
        "te,de->td", logit_grad, router_weight.astype(jnp.float32), precision=lax.Precision.HIGHEST
    )
    token_grad = (jnp.sum(grad_sel.astype(jnp.float32), axis=1) + router_back).astype(jnp.bfloat16)
    return (layer_out, token_grad, gate_grad, up_grad, down_grad, router_grad)


def swap(array, bit):
    if bit == 0:
        return lax.ppermute(array, "dp", [(0, 1), (1, 0)])
    size = lax.axis_size("expert")
    return lax.ppermute(array, "expert", [(i, i ^ bit) for i in range(size)])


def local_dense(tokens, routes, cotangent, router_weight, gate_weight, up_weight, down_weight):
    tok_rows = tokens.shape[0]
    model_width = tokens.shape[1]
    expert_count = router_weight.shape[1]
    group_size = lax.axis_size("expert")
    dp_size = lax.axis_size("dp")
    dp_index = lax.axis_index("dp")
    expert_index = lax.axis_index("expert")
    gate_mat, up_mat, down_mat = gate_weight[0], up_weight[0], down_weight[0]
    logits = jnp.dot(tokens, router_weight, preferred_element_type=jnp.float32)
    exp_logits = jnp.exp(logits)
    probability = exp_logits / jnp.sum(exp_logits, axis=1, keepdims=True)
    chosen = jnp.sum(
        (routes[:, :, None] == jnp.arange(expert_count, dtype=jnp.int32)[None, None, :]).astype(
            jnp.float32
        ),
        axis=1,
    )
    selected = chosen * probability
    sel_total = jnp.sum(selected, axis=1, keepdims=True)
    combine = selected / sel_total
    bits = [1, 0, 2, 8, 4]
    ones = (1,) * len(bits)

    def gather(array, order):
        array = array.reshape(ones + array.shape)
        for bit in order:
            array = jnp.concatenate([array, swap(array, bit)], axis=bits.index(bit))
        return array.reshape((-1, array.shape[-1]))

    combine_all = gather(combine, (4, 8, 2, 0, 1))
    tokens_all = gather(tokens, (4, 8, 2, 0, 1))
    cot_all = gather(cotangent, (4, 8, 0, 2, 1))
    mine = (jnp.arange(expert_count, dtype=jnp.int32) == expert_index).astype(jnp.float32)
    scale = jnp.sum(combine_all * mine[None, :], axis=1, keepdims=True)
    gate_act = jnp.dot(tokens_all, gate_mat, preferred_element_type=jnp.float32)
    up_act = jnp.dot(tokens_all, up_mat, preferred_element_type=jnp.float32)
    raw_grad = lax.dot_general(
        cot_all, down_mat, (((1,), (1,)), ((), ())), preferred_element_type=jnp.float32
    )
    act_value, act_slope = silu_parts(gate_act)
    hidden = act_value * up_act
    comb_mine = jnp.sum(hidden * raw_grad, axis=1)
    scaled_hidden = (hidden * scale).astype(jnp.bfloat16)
    hidden_grad = raw_grad * scale
    gate_part = (hidden_grad * up_act * act_slope).astype(jnp.bfloat16)
    up_part = (hidden_grad * act_value).astype(jnp.bfloat16)

    def rows_of(array):
        quarter = array.reshape((2, 2, group_size * tok_rows // 2) + array.shape[1:])
        return quarter[:, 0].reshape((group_size * tok_rows,) + array.shape[1:])

    def scatter(term):
        term = term.reshape((2, 2, 2, 2, tok_rows, model_width))
        for bit in (1, 2, 8, 4):
            total = term[0].astype(jnp.float32) + swap(term[1], bit).astype(jnp.float32)
            term = total.astype(jnp.bfloat16)
        return total

    out_term = jnp.dot(
        rows_of(scaled_hidden), down_mat, preferred_element_type=jnp.float32
    ).astype(jnp.bfloat16)
    in_term = (
        lax.dot_general(
            rows_of(gate_part), gate_mat, (((1,), (1,)), ((), ())),
            preferred_element_type=jnp.float32,
        )
        + lax.dot_general(
            rows_of(up_part), up_mat, (((1,), (1,)), ((), ())),
            preferred_element_type=jnp.float32,
        )
    ).astype(jnp.bfloat16)
    layer_out = scatter(out_term).astype(jnp.bfloat16)
    in_sum = scatter(in_term)
    part_width = model_width // dp_size
    start = dp_index * part_width
    tokens_part = lax.dynamic_slice_in_dim(tokens_all, start, part_width, axis=1)
    cot_part = lax.dynamic_slice_in_dim(cot_all, start, part_width, axis=1)
    over_rows = (((0,), (0,)), ((), ()))
    gate_grad = lax.dot_general(
        tokens_part, gate_part, over_rows, preferred_element_type=jnp.float32
    ).astype(jnp.bfloat16)
    up_grad = lax.dot_general(
        tokens_part, up_part, over_rows, preferred_element_type=jnp.float32
    ).astype(jnp.bfloat16)
    down_grad = lax.dot_general(
        scaled_hidden, cot_part, over_rows, preferred_element_type=jnp.float32
    ).astype(jnp.bfloat16)
    comb = rows_of(comb_mine).reshape((2, 2, 2, 2, tok_rows, 1))
    places = []
    for step, bit in enumerate((1, 2, 8, 4)):
        comb = jnp.concatenate([comb[0], swap(comb[1], bit)], axis=-1)
        places = places + [p + bit for p in places] if step else [0, bit]
    columns = jnp.asarray(places, jnp.int32) ^ expert_index
    spread = (
        columns[:, None] == jnp.arange(expert_count, dtype=jnp.int32)[None, :]
    ).astype(jnp.float32)
    comb_grad = jnp.sum(comb[:, :, None] * spread[None], axis=1)
    sel_grad = (
        chosen * (comb_grad - jnp.sum(combine * comb_grad, axis=1, keepdims=True)) / sel_total
    )
    logit_grad = probability * (sel_grad - jnp.sum(probability * sel_grad, axis=1, keepdims=True))
    router_term = jnp.einsum(
        "td,te->de", tokens.astype(jnp.float32), logit_grad, precision=lax.Precision.HIGHEST
    )
    router_grad = lax.psum(router_term, ("dp", "expert"))
    router_back = jnp.einsum(
        "te,de->td", logit_grad, router_weight.astype(jnp.float32), precision=lax.Precision.HIGHEST
    )
    token_grad = (in_sum + router_back).astype(jnp.bfloat16)
    return (layer_out, token_grad, gate_grad[None], up_grad[None], down_grad[None], router_grad)


def local(tokens, routes, cotangent, router_weight, gate_weight, up_weight, down_weight):
    tok_rows, top_count = routes.shape
    capacity = min(tok_rows, 2 * tok_rows * top_count // router_weight.shape[1])
    dense = (
        capacity == tok_rows
        and gate_weight.shape[0] == 1
        and lax.axis_size("dp") == 2
        and lax.axis_size("expert") == 16
    )
    plan = local_dense if dense else local_slots
    return plan(tokens, routes, cotangent, router_weight, gate_weight, up_weight, down_weight)


def solution(mesh):
    return jax.shard_map(
        local,
        mesh=mesh,
        in_specs=(
            P(("dp", "expert"), None),
            P(("dp", "expert"), None),
            P(("dp", "expert"), None),
            P(),
            P("expert", None, None),
            P("expert", None, None),
            P("expert", None, None),
        ),
        out_specs=(
            P(("dp", "expert"), None),
            P(("dp", "expert"), None),
            P("expert", "dp", None),
            P("expert", "dp", None),
            P("expert", None, "dp"),
            P(),
        ),
        check_vma=False,
    )
```

```python
import jax
import jax.numpy as jnp
from jax import lax
from jax.sharding import PartitionSpec as P


def silu_parts(gate_act):
    sigmoid_value = jax.nn.sigmoid(gate_act)
    act_value = gate_act * sigmoid_value
    act_slope = sigmoid_value * (1.0 + gate_act * (1.0 - sigmoid_value))
    return (act_value, act_slope)


def expert_forward(arrived, gate_weight, up_weight, down_weight):
    gate_act = jnp.einsum(
        "sjcd,jdf->sjcf", arrived, gate_weight, preferred_element_type=jnp.float32
    )
    up_act = jnp.einsum("sjcd,jdf->sjcf", arrived, up_weight, preferred_element_type=jnp.float32)
    act_value, act_slope = silu_parts(gate_act)
    hidden = (act_value * up_act).astype(jnp.bfloat16)
    expert_out = jnp.einsum(
        "sjcf,jfd->sjcd", hidden, down_weight, preferred_element_type=jnp.float32
    ).astype(jnp.bfloat16)
    return (expert_out, (up_act, act_value, act_slope, hidden))


def expert_backward(arrived_grads, stored, gate_weight, up_weight, down_weight):
    up_act, act_value, act_slope, hidden = stored
    hidden_grad = jnp.einsum(
        "sjcd,jfd->sjcf", arrived_grads, down_weight, preferred_element_type=jnp.float32
    )
    gate_part = (hidden_grad * up_act * act_slope).astype(jnp.bfloat16)
    up_part = (hidden_grad * act_value).astype(jnp.bfloat16)
    input_grad = (
        jnp.einsum("sjcf,jdf->sjcd", gate_part, gate_weight, preferred_element_type=jnp.float32)
        + jnp.einsum("sjcf,jdf->sjcd", up_part, up_weight, preferred_element_type=jnp.float32)
    ).astype(jnp.bfloat16)
    return (input_grad, gate_part, up_part)


def local_slots(tokens, routes, cotangent, router_weight, gate_weight, up_weight, down_weight):
    tok_rows, top_count = routes.shape
    model_width = tokens.shape[1]
    expert_count = router_weight.shape[1]
    local_count = gate_weight.shape[0]
    group_size = lax.axis_size("expert")
    capacity = min(tok_rows, 2 * tok_rows * top_count // expert_count)
    slot_total = expert_count * capacity
    buffer_shape = (group_size, local_count, capacity, model_width)
    logits = jnp.dot(tokens, router_weight, preferred_element_type=jnp.float32)
    exp_logits = jnp.exp(logits)
    probability = exp_logits / jnp.sum(exp_logits, axis=1, keepdims=True)
    chosen = (
        routes[:, :, None] == jnp.arange(expert_count, dtype=jnp.int32)[None, None, :]
    ).astype(jnp.int32)
    chosen_float = chosen.astype(jnp.float32)
    selected = jnp.sum(chosen_float * probability[:, None, :], axis=2)
    sel_total = jnp.sum(selected, axis=1, keepdims=True)
    combine = selected / sel_total
    per_token = jnp.sum(chosen, axis=1)
    before = jnp.tril(jnp.ones((tok_rows, tok_rows), jnp.float32), -1)
    earlier = jnp.dot(before, per_token.astype(jnp.float32)).astype(jnp.int32)
    slot_ids = jnp.sum(chosen * earlier[:, None, :], axis=2)
    flat_slot = routes * capacity + slot_ids
    match_map = (
        flat_slot[:, :, None] == jnp.arange(slot_total, dtype=jnp.int32)[None, None, :]
    ).astype(jnp.float32)
    presence = jnp.sum(match_map, axis=1)
    weight_map = jnp.sum(match_map * combine[:, :, None], axis=1)
    send_rows = (
        jnp.einsum(
            "tr,td->rd", presence.astype(jnp.bfloat16), tokens, preferred_element_type=jnp.float32
        )
        .astype(jnp.bfloat16)
        .reshape(buffer_shape)
    )
    send_grads = (
        jnp.einsum(
            "tr,td->rd", weight_map, cotangent.astype(jnp.float32), precision=lax.Precision.HIGHEST
        )
        .astype(jnp.bfloat16)
        .reshape(buffer_shape)
    )
    arrived = lax.all_to_all(send_rows, "expert", split_axis=0, concat_axis=0, tiled=True)
    expert_out, stored = expert_forward(arrived, gate_weight, up_weight, down_weight)
    returned = lax.all_to_all(expert_out, "expert", split_axis=0, concat_axis=0, tiled=True)
    arrived_grads = lax.all_to_all(send_grads, "expert", split_axis=0, concat_axis=0, tiled=True)
    input_grad, gate_part, up_part = expert_backward(
        arrived_grads, stored, gate_weight, up_weight, down_weight
    )
    returned_grads = lax.all_to_all(input_grad, "expert", split_axis=0, concat_axis=0, tiled=True)
    hidden = stored[3]
    gate_term = jnp.einsum("sjcd,sjcf->jdf", arrived, gate_part, preferred_element_type=jnp.float32)
    up_term = jnp.einsum("sjcd,sjcf->jdf", arrived, up_part, preferred_element_type=jnp.float32)
    down_term = jnp.einsum(
        "sjcf,sjcd->jfd", hidden, arrived_grads, preferred_element_type=jnp.float32
    )
    gate_sum, up_sum, down_sum = (
        lax.psum_scatter(gate_term, "dp", scatter_dimension=1, tiled=True),
        lax.psum_scatter(up_term, "dp", scatter_dimension=1, tiled=True),
        lax.psum_scatter(down_term, "dp", scatter_dimension=2, tiled=True),
    )
    gate_grad = gate_sum.astype(jnp.bfloat16)
    up_grad = up_sum.astype(jnp.bfloat16)
    down_grad = down_sum.astype(jnp.bfloat16)
    flat_index = flat_slot.reshape(-1)
    out_sel = jnp.take(returned.reshape(slot_total, model_width), flat_index, axis=0).reshape(
        tok_rows, top_count, model_width
    )
    grad_sel = jnp.take(
        returned_grads.reshape(slot_total, model_width), flat_index, axis=0
    ).reshape(tok_rows, top_count, model_width)
    layer_out = jnp.sum(combine[:, :, None] * out_sel.astype(jnp.float32), axis=1).astype(
        jnp.bfloat16
    )
    comb_grad = jnp.einsum("tkd,td->tk", out_sel, cotangent, preferred_element_type=jnp.float32)
    sel_grad = (comb_grad - jnp.sum(combine * comb_grad, axis=1, keepdims=True)) / sel_total
    prob_grad = jnp.sum(chosen_float * sel_grad[:, :, None], axis=1)
    logit_grad = probability * (prob_grad - jnp.sum(probability * prob_grad, axis=1, keepdims=True))
    router_term = jnp.einsum(
        "td,te->de", tokens.astype(jnp.float32), logit_grad, precision=lax.Precision.HIGHEST
    )
    router_grad = lax.psum(router_term, ("dp", "expert"))
    router_back = jnp.einsum(
        "te,de->td", logit_grad, router_weight.astype(jnp.float32), precision=lax.Precision.HIGHEST
    )
    token_grad = (jnp.sum(grad_sel.astype(jnp.float32), axis=1) + router_back).astype(jnp.bfloat16)
    return (layer_out, token_grad, gate_grad, up_grad, down_grad, router_grad)


def swap(array, bit):
    if bit == 0:
        return lax.ppermute(array, "dp", [(0, 1), (1, 0)])
    size = lax.axis_size("expert")
    return lax.ppermute(array, "expert", [(i, i ^ bit) for i in range(size)])


def local_dense(tokens, routes, cotangent, router_weight, gate_weight, up_weight, down_weight):
    tok_rows = tokens.shape[0]
    model_width = tokens.shape[1]
    expert_count = router_weight.shape[1]
    group_size = lax.axis_size("expert")
    dp_size = lax.axis_size("dp")
    dp_index = lax.axis_index("dp")
    expert_index = lax.axis_index("expert")
    gate_mat, up_mat, down_mat = gate_weight[0], up_weight[0], down_weight[0]
    logits = jnp.dot(tokens, router_weight, preferred_element_type=jnp.float32)
    exp_logits = jnp.exp(logits)
    probability = exp_logits / jnp.sum(exp_logits, axis=1, keepdims=True)
    chosen = jnp.sum(
        (routes[:, :, None] == jnp.arange(expert_count, dtype=jnp.int32)[None, None, :]).astype(
            jnp.float32
        ),
        axis=1,
    )
    selected = chosen * probability
    sel_total = jnp.sum(selected, axis=1, keepdims=True)
    combine = selected / sel_total
    bits = [1, 0, 2, 8, 4]
    ones = (1,) * len(bits)

    def gather(array, order):
        array = array.reshape(ones + array.shape)
        for bit in order:
            array = jnp.concatenate([array, swap(array, bit)], axis=bits.index(bit))
        return array.reshape((-1, array.shape[-1]))

    combine_all = gather(combine, (4, 8, 2, 0, 1))
    tokens_all = gather(tokens, (4, 8, 2, 0, 1))
    cot_all = gather(cotangent, (4, 8, 0, 2, 1))
    mine = (jnp.arange(expert_count, dtype=jnp.int32) == expert_index).astype(jnp.float32)
    scale = jnp.sum(combine_all * mine[None, :], axis=1, keepdims=True)
    gate_act = jnp.dot(tokens_all, gate_mat, preferred_element_type=jnp.float32)
    up_act = jnp.dot(tokens_all, up_mat, preferred_element_type=jnp.float32)
    raw_grad = lax.dot_general(
        cot_all, down_mat, (((1,), (1,)), ((), ())), preferred_element_type=jnp.float32
    )
    act_value, act_slope = silu_parts(gate_act)
    hidden = act_value * up_act
    comb_mine = jnp.sum(hidden * raw_grad, axis=1)
    scaled_hidden = (hidden * scale).astype(jnp.bfloat16)
    hidden_grad = raw_grad * scale
    gate_part = (hidden_grad * up_act * act_slope).astype(jnp.bfloat16)
    up_part = (hidden_grad * act_value).astype(jnp.bfloat16)

    def rows_of(array):
        quarter = array.reshape((2, 2, group_size * tok_rows // 2) + array.shape[1:])
        return quarter[:, 0].reshape((group_size * tok_rows,) + array.shape[1:])

    def scatter(term):
        term = term.reshape((2, 2, 2, 2, tok_rows, model_width))
        for bit in (1, 2, 8, 4):
            total = term[0].astype(jnp.float32) + swap(term[1], bit).astype(jnp.float32)
            term = total.astype(jnp.bfloat16)
        return total

    out_term = jnp.dot(
        rows_of(scaled_hidden), down_mat, preferred_element_type=jnp.float32
    ).astype(jnp.bfloat16)
    in_term = (
        lax.dot_general(
            rows_of(gate_part), gate_mat, (((1,), (1,)), ((), ())),
            preferred_element_type=jnp.float32,
        )
        + lax.dot_general(
            rows_of(up_part), up_mat, (((1,), (1,)), ((), ())),
            preferred_element_type=jnp.float32,
        )
    ).astype(jnp.bfloat16)
    layer_out = scatter(out_term).astype(jnp.bfloat16)
    in_sum = scatter(in_term)
    part_width = model_width // dp_size
    start = dp_index * part_width
    tokens_part = lax.dynamic_slice_in_dim(tokens_all, start, part_width, axis=1)
    cot_part = lax.dynamic_slice_in_dim(cot_all, start, part_width, axis=1)
    over_rows = (((0,), (0,)), ((), ()))
    gate_grad = lax.dot_general(
        tokens_part, gate_part, over_rows, preferred_element_type=jnp.float32
    ).astype(jnp.bfloat16)
    up_grad = lax.dot_general(
        tokens_part, up_part, over_rows, preferred_element_type=jnp.float32
    ).astype(jnp.bfloat16)
    down_grad = lax.dot_general(
        scaled_hidden, cot_part, over_rows, preferred_element_type=jnp.float32
    ).astype(jnp.bfloat16)
    comb = rows_of(comb_mine).reshape((2, 2, 2, 2, tok_rows, 1))
    places = []
    for step, bit in enumerate((1, 2, 8, 4)):
        comb = jnp.concatenate([comb[0], swap(comb[1], bit)], axis=-1)
        places = places + [p + bit for p in places] if step else [0, bit]
    columns = jnp.asarray(places, jnp.int32) ^ expert_index
    spread = (
        columns[:, None] == jnp.arange(expert_count, dtype=jnp.int32)[None, :]
    ).astype(jnp.float32)
    comb_grad = jnp.sum(comb[:, :, None] * spread[None], axis=1)
    sel_grad = (
        chosen * (comb_grad - jnp.sum(combine * comb_grad, axis=1, keepdims=True)) / sel_total
    )
    logit_grad = probability * (sel_grad - jnp.sum(probability * sel_grad, axis=1, keepdims=True))
    router_term = jnp.einsum(
        "td,te->de", tokens.astype(jnp.float32), logit_grad, precision=lax.Precision.HIGHEST
    )
    router_grad = router_term
    for bit in (1, 2, 0, 8, 4):
        router_grad = router_grad + swap(router_grad, bit)
    router_back = jnp.einsum(
        "te,de->td", logit_grad, router_weight.astype(jnp.float32), precision=lax.Precision.HIGHEST
    )
    token_grad = (in_sum + router_back).astype(jnp.bfloat16)
    return (layer_out, token_grad, gate_grad[None], up_grad[None], down_grad[None], router_grad)


def local(tokens, routes, cotangent, router_weight, gate_weight, up_weight, down_weight):
    tok_rows, top_count = routes.shape
    capacity = min(tok_rows, 2 * tok_rows * top_count // router_weight.shape[1])
    dense = (
        capacity == tok_rows
        and gate_weight.shape[0] == 1
        and lax.axis_size("dp") == 2
        and lax.axis_size("expert") == 16
    )
    plan = local_dense if dense else local_slots
    return plan(tokens, routes, cotangent, router_weight, gate_weight, up_weight, down_weight)


def solution(mesh):
    return jax.shard_map(
        local,
        mesh=mesh,
        in_specs=(
            P(("dp", "expert"), None),
            P(("dp", "expert"), None),
            P(("dp", "expert"), None),
            P(),
            P("expert", None, None),
            P("expert", None, None),
            P("expert", None, None),
        ),
        out_specs=(
            P(("dp", "expert"), None),
            P(("dp", "expert"), None),
            P("expert", "dp", None),
            P("expert", "dp", None),
            P("expert", None, "dp"),
            P(),
        ),
        check_vma=False,
    )
```
